32 devices in a mesh: parts: 2 (over y), member: 4 (over z), tile: 4 (over x, core).
Axes of the slice: x: 2, y: 2, z: 4, core: 2. Of those that a mesh axis runs over, the one named last changes fastest.
Arguments:
- state: float32 [8, 3, 20, 16, 1024], P(('parts', 'member'), None, None, 'tile'), parts along dimension 0, may hold values from -3 to 3
- parent: int32 [8], P('parts'), parts along dimension 0, may hold values from 0 to 3
- depth: float32 [20], replicated, may hold values from 0.1 to 1
- interp: bfloat16 [8, 128, 4096], P(('parts', 'tile')), parts along dimension 0, may hold values from -0.09375 to 0.09375
- obs: float32 [8, 2, 128], P(('parts', 'tile')), parts along dimension 0, may hold values from -6 to 6
- counts: int32 [8], P(('parts', 'tile')), parts along dimension 0, may hold values from 1 to 128, 256 in all
Outputs:
- predicted_states: float32 [8, 3, 20, 16, 1024], P(('parts', 'member'), None, None, 'tile'), parts along dimension 0
- tracker_mismatch: float32 [8], P(('parts', 'member')), parts along dimension 0
The draws below stay inside these ranges and needn't reach their ends.
There are 2 independent parts, one for each index of `parts`. The reference program is written for one: setup_inputs(seed, part) draws one part's arguments, and reference() takes and returns one part's arrays. A program takes and returns all parts, laid end to end along the dimension named above; an argument that names none is the same for every part. Nothing has to cross between parts.
All inputs are finite; a program needn't handle non-finite values. No bound on the sum of `counts` on one device may be relied on, other than what follows from the above.
Results may differ from the reference program's by a relative error of at most 0.00069.
Values sent between devices are 32-bit elements; how exact they have to be, the bound alone decides.
A program may use at most 64 MiB of HBM per device.

```python
import math
import jax
import jax.numpy as jnp
import numpy as np
from jax import lax

CX = 4
CY = 1024
LEVELS = 20
OBS = 128
STEPS = 4
ENSEMBLE_SIZE = 4
TILES = 4
NX = 16


def plant(array, rng, low, high):
    longest = array.shape.index(max(array.shape))
    spots = []
    for shift in (0, 1):
        where = [jax.random.randint(jax.random.fold_in(rng, axis), (), 0, length) for axis, length in enumerate(array.shape)]
        where[longest] = (where[longest] + shift) % array.shape[longest]
        spots.append(tuple(where))
    return array.at[spots[0]].set(low).at[spots[1]].set(high)


def block_scale(key, extent, cuts, low, largest):
    def one(axis_at, parts):
        heights = jax.random.uniform(jax.random.fold_in(jax.random.fold_in(key, 6), axis_at), (parts,), jnp.float32, low / len(cuts), largest / len(cuts))
        return jnp.repeat(jnp.exp(heights), extent[axis_at] // parts).reshape((-1,) + (1,) * (len(extent) - axis_at - 1))

    gain = one(*cuts[0])
    for cut in cuts[1:]:
        gain = gain * one(*cut)
    return gain


def rank_bounds(count, slope):
    loads = [(1 << 20) // math.isqrt(rank ** slope) + 1 for rank in range(1, count + 1)]
    width = 1 + sum(loads) // (1 << 30)
    return np.cumsum(np.array([max(1, weight // width) for weight in loads]))


def ranked(rng, dims, amount, slope):
    listing = rank_bounds(amount, slope)
    pick = jax.random.randint(jax.random.fold_in(rng, 1), dims, 0, int(listing[amount - 1]))
    grade = jnp.searchsorted(jnp.asarray(listing, jnp.int32), pick, side="right")
    return jax.random.permutation(jax.random.fold_in(rng, 2), amount)[grade].astype(jnp.int32)


def profile(amount, total, limit, lean):
    weights = [(1 << 20) // math.isqrt(standing ** lean) + 1 for standing in range(2, amount + 1)]
    surplus, given = total - limit - (amount - 1), [1] * (amount - 1)
    while surplus > 0:
        movable = [i for i in range(amount - 1) if given[i] < limit]
        pool, remaining = sum([weights[i] for i in movable]), surplus
        for i in movable:
            extra = min(limit - given[i], max(1, remaining * weights[i] // pool), surplus)
            given[i] = given[i] + extra
            surplus = surplus - extra
    return np.array([limit] + given)


def uneven(key, count, total, limit, lean):
    if count == 2:
        one = jax.random.randint(key, (), max(1, total - limit), min(limit, total - 1) + 1)
        return jnp.stack([one, total - one])
    sizes = jnp.asarray(profile(count, total, limit, lean), jnp.int32)
    couples = (count - 1) // 2
    source_of, sink = sizes[1:1 + 2 * couples:2], sizes[2:2 + 2 * couples:2]
    margin = jnp.minimum(source_of - 1, limit - sink)
    passed = jax.random.randint(jax.random.fold_in(key, 1), (couples,), 0, 1 << 20) % (margin + 1)
    sizes = sizes.at[1:1 + 2 * couples:2].set(source_of - passed).at[2:2 + 2 * couples:2].set(sink + passed)
    return sizes[jax.random.permutation(jax.random.fold_in(key, 2), count)]


def centred(key, extent, scale, limit, shards=(), held_as=jnp.bfloat16):
    factor_of = block_scale(key, extent, shards, -0.22, 0.18) if shards else 1.0
    entries = jax.random.normal(key, extent, jnp.float32) * scale * factor_of
    return jnp.minimum(jnp.maximum(entries, -limit), limit).astype(held_as)


def setup_inputs(seed: int = 0, part: int = 0) -> dict:
    splits = jax.random.split(jax.random.key(seed), 7)
    part_keys = jax.random.split(jax.random.fold_in(splits[6], part), 7)
    return {
        "state": centred(part_keys[0], (ENSEMBLE_SIZE, 3, LEVELS, NX, CY), 0.5, 3.0, ((0, 4), (3, 4)), jnp.float32),
        "parent": plant(ranked(part_keys[1], (ENSEMBLE_SIZE,), ENSEMBLE_SIZE, 2), jax.random.fold_in(part_keys[1], 3), 0, ENSEMBLE_SIZE - 1).astype(jnp.int32),
        "depth": jnp.clip(jnp.exp(jax.random.uniform(splits[2], (LEVELS,), jnp.float32, math.log(0.1), math.log(1.0))), 0.1, 1.0),
        "interp": centred(part_keys[3], (TILES, OBS, CX * CY), (CX * CY) ** -0.5, 0.09375, ((0, 4),)),
        "obs": centred(part_keys[4], (TILES, 2, OBS), 1.0, 6.0, ((0, 4),), jnp.float32),
        "counts": uneven(part_keys[5], TILES, OBS * TILES // 2, OBS, 2).astype(jnp.int32),
    }


time_step = 0.3
nudge_gain = 2.0
coriolis = 0.5
viscosity = 0.05
mixing = 0.1


def shift_cols(field, nudge_quantity):
    return jnp.roll(field, nudge_quantity, axis=2)


def vertical_mix(field):
    padded = jnp.concatenate([field[:1], field, field[-1:]], axis=0)
    return mixing * (padded[2:] + padded[:-2] - 2.0 * field)


def forward_step(extended, depth):
    u_ext, v_ext, h_ext = extended[0], extended[1], extended[2]

    def eastward_difference(field):
        return (field[:, 2:] - field[:, :-2]) * 0.5

    def diff_y(field):
        return (shift_cols(field, -1) - shift_cols(field, 1)) * 0.5

    def laplace(field):
        inner = field[:, 1:-1]
        return field[:, 2:] + field[:, :-2] + shift_cols(inner, -1) + shift_cols(inner, 1) - 4.0 * inner

    u_core = u_ext[:, 1:-1]
    v_core = v_ext[:, 1:-1]
    interior_height = h_ext[:, 1:-1]
    u_next = u_core + time_step * (coriolis * v_core - eastward_difference(h_ext) + viscosity * laplace(u_ext) + vertical_mix(u_core))
    v_next = v_core + time_step * (-coriolis * u_core - diff_y(interior_height) + viscosity * laplace(v_ext) + vertical_mix(v_core))
    h_next = h_ext[:, 2:-2] - time_step * depth[:, None, None] * (eastward_difference(u_next) + diff_y(v_next[:, 1:-1]))
    return jnp.stack([u_next[:, 1:-1], v_next[:, 1:-1], h_next])


def observation_residual(fields, interp, obs, live):
    surf = fields[0:2, 0].reshape(2, TILES, CX * CY).astype(jnp.bfloat16)
    pred = jnp.einsum("ktc,toc->tko", surf.astype(jnp.float32), interp.astype(jnp.float32))
    return live * (obs - pred)


def reference(state, parent, depth, interp, obs, counts):
    live = (jnp.arange(OBS, dtype=jnp.int32)[None, :] < counts[:, None]).astype(jnp.float32)[:, None, :]
    chosen_ancestors = jnp.take(state, parent, axis=0)

    def lone_realization(fields):
        for step in range(STEPS):
            innov = observation_residual(fields, interp, obs, live)
            back = jnp.einsum("tko,toc->ktc", innov.astype(jnp.bfloat16).astype(jnp.float32), interp.astype(jnp.float32))
            fields = fields.at[0:2, 0].add(time_step * nudge_gain * back.reshape(2, NX, CY))
            extended = jnp.pad(fields, ((0, 0), (0, 0), (2, 2), (0, 0)))
            fields = forward_step(extended, depth)
        innov = observation_residual(fields, interp, obs, live)
        return fields, 0.5 * jnp.sum(innov * innov)

    predicted_states, tracker_mismatch = lax.map(lone_realization, chosen_ancestors)
    return predicted_states, tracker_mismatch
```

```python
import functools

import jax
import jax.numpy as jnp
from jax import lax
from jax.experimental import pallas as pl
from jax.experimental.pallas import tpu as pltpu
from jax.sharding import PartitionSpec as P

STEPS = 4
U, H, V = 0, 1, 2
SOURCE = {U: 0, V: 1, H: 2}
MESH = pl.DeviceIdType.MESH

time_step = 0.3
nudge_gain = 2.0
coriolis = 0.5
viscosity = 0.05
mixing = 0.1


def west(field):
    turned = pltpu.roll(field, 1, 2)
    wrapped = pltpu.roll(turned, 1, 1)
    lane = lax.broadcasted_iota(jnp.int32, field.shape, 2)
    return jnp.where(lane == 0, wrapped, turned)


def east(field):
    turned = pltpu.roll(field, 127, 2)
    wrapped = pltpu.roll(turned, 7, 1)
    lane = lax.broadcasted_iota(jnp.int32, field.shape, 2)
    return jnp.where(lane == 127, wrapped, turned)


def forecast_kernel(
    levels, tiles,
    state, depth, interp, obs, counts,
    out, misfit,
    x, terms, send_sem, recv_sem, term_send, term_recv,
):
    tile = lax.axis_index("tile")
    right, left = lax.rem(tile + 1, tiles), lax.rem(tile + tiles - 1, tiles)
    barrier = pltpu.get_barrier_semaphore()
    for hop in range(1, tiles):
        pl.semaphore_signal(
            barrier, inc=1, device_id={"tile": lax.rem(tile + hop, tiles)}, device_id_type=MESH
        )

    split = [levels // 2 - 1 + t for t in range(STEPS + 1)]

    def span(group, t):
        return (split[t], levels) if group == 0 else (0, split[t])

    def raw(f, l, r):
        return pl.ds((SOURCE[f] * levels + l) * 32 + r, 8, stride=4)

    def load(group):
        low, high = span(group, 0)

        @pl.loop(low, high)
        def _(l):
            for f in (U, H, V):
                for r in range(4):
                    x[0, f, l, 2 + r] = state[raw(f, l, r), :]

    def halo(group, t, side):
        low, high = span(group, t)
        lv = pl.ds(low, high - low)
        if side == 0:
            pieces = ((x.at[t, pl.ds(0, 2), lv, pl.ds(4, 2)], x.at[t, pl.ds(0, 2), lv, pl.ds(0, 2)]),
                      (x.at[t, V, lv, pl.ds(5, 1)], x.at[t, V, lv, pl.ds(1, 1)]))
            to = right
        else:
            pieces = ((x.at[t, pl.ds(0, 2), lv, pl.ds(2, 2)], x.at[t, pl.ds(0, 2), lv, pl.ds(6, 2)]),
                      (x.at[t, V, lv, pl.ds(2, 1)], x.at[t, V, lv, pl.ds(6, 1)]))
            to = left
        return [
            pltpu.make_async_remote_copy(
                src_ref=src, dst_ref=dst,
                send_sem=send_sem.at[t, group, side, i], recv_sem=recv_sem.at[t, group, side, i],
                device_id={"tile": to}, device_id_type=MESH,
            )
            for i, (src, dst) in enumerate(pieces)
        ]

    sends = (tile < tiles - 1, tile > 0)
    receives = (tile > 0, tile < tiles - 1)

    def send(group, t):
        for side in (0, 1):
            @pl.when(sends[side])
            def _():
                for copy in halo(group, t, side):
                    copy.start()

    def arrived(group, t):
        for side in (0, 1):
            @pl.when(receives[side])
            def _():
                for copy in halo(group, t, side):
                    copy.wait_recv()

    def cell(t, l, below, above):
        u, h = x[t, U, l], x[t, H, l]
        v = x[t, V, l, 1:7]
        core = u[1:7]
        u1 = (
            (1.0 - time_step * (4.0 * viscosity + 2.0 * mixing)) * core
            + (time_step * coriolis) * v
            - (time_step * 0.5) * (h[2:8] - h[0:6])
            + (time_step * viscosity) * ((u[2:8] + u[0:6]) + (west(core) + east(core)))
            + (time_step * mixing) * (x[t, U, below, 1:7] + x[t, U, above, 1:7])
        )
        mid = v[1:5]
        diffuse = (time_step * viscosity) * mid
        slope = (time_step * 0.5) * h[2:6]
        v1 = (
            (1.0 - time_step * (4.0 * viscosity + 2.0 * mixing)) * mid
            - (time_step * coriolis) * u[2:6]
            + (time_step * viscosity) * (v[2:6] + v[0:4])
            + (east(diffuse - slope) + west(diffuse + slope))
            + (time_step * mixing) * (x[t, V, below, 2:6] + x[t, V, above, 2:6])
        )
        h1 = h[2:6] - (time_step * 0.5 * depth[l]) * (
            (u1[2:6] - u1[0:4]) + (east(v1) - west(v1))
        )
        x[t + 1, U, l, 2:6] = u1[1:5]
        x[t + 1, V, l, 2:6] = v1
        x[t + 1, H, l, 2:6] = h1

    def advance(group, t):
        low, high = span(group, t + 1)
        if low == 0:
            cell(t, 0, 0, 1)
            low = 1
        last = high == levels
        if last:
            high = levels - 1

        @pl.loop(low, high)
        def _(l):
            cell(t, l, l - 1, l + 1)

        if last:
            cell(t, levels - 1, levels - 2, levels - 1)

    row = lax.broadcasted_iota(jnp.int32, (8, 128), 0)
    live = lax.broadcasted_iota(jnp.int32, (1, 128), 1) < counts[0]

    def residual(t):
        pieces = []
        for r in range(4):
            u, v = x[t, U, 0, 2 + r], x[t, V, 0, 2 + r]
            for block in range(8):
                here = row == block
                pieces.append(
                    jnp.concatenate([jnp.where(here, u, 0.0), jnp.where(here, v, 0.0)], axis=0)
                    .astype(jnp.bfloat16)
                )
        surf = jnp.concatenate(pieces, axis=1)
        pred = lax.dot_general(
            surf, interp[...], (((1,), (1,)), ((), ())), preferred_element_type=jnp.float32
        )
        result = []
        for k in (0, 1):
            whole = jnp.sum(pred[8 * k:8 * k + 8], axis=0, keepdims=True)
            result.append(jnp.where(live, obs[k:k + 1, :] - whole, 0.0))
        return result

    def nudge(t):
        innov = jnp.concatenate(
            [jnp.broadcast_to(part, (8, 128)) for part in residual(t)], axis=0
        ).astype(jnp.bfloat16)
        back = jnp.dot(innov, interp[...], preferred_element_type=jnp.float32)
        for k, f in ((0, U), (1, V)):
            for r in range(4):
                total = jnp.zeros((8, 128), jnp.float32)
                for block in range(8):
                    at = (r * 8 + block) * 128
                    total = jnp.where(row == block, back[8 * k:8 * k + 8, at:at + 128], total)
                x[t, f, 0, 2 + r] += (time_step * nudge_gain) * total

    def store(group):
        low, high = span(group, STEPS)

        @pl.loop(low, high)
        def _(l):
            for f in (U, H, V):
                for r in range(4):
                    out[raw(f, l, r), :] = x[STEPS, f, l, 2 + r]

    for side, rows in ((0, 0), (1, 6)):
        @pl.when(jnp.logical_not(receives[side]))
        def _():
            @pl.loop(0, levels)
            def _(l):
                for t in range(STEPS):
                    for f in (U, H, V):
                        x[t, f, l, rows:rows + 2] = jnp.zeros((2, 8, 128), jnp.float32)

    load(0)
    pl.semaphore_wait(barrier, tiles - 1)
    send(0, 0)
    load(1)
    nudge(0)
    send(1, 0)
    for t in range(STEPS):
        for group in (0, 1):
            arrived(group, t)
            advance(group, t)
            if t + 1 < STEPS:
                if group == 1:
                    nudge(t + 1)
                send(group, t + 1)
            else:
                store(group)

    part_u, part_v = residual(STEPS)
    terms[pl.ds(tile, 1)] = jnp.broadcast_to(
        0.5 * (part_u * part_u + part_v * part_v), (1, 8, 128)
    )
    copies = []
    for hop in range(1, tiles):
        copies.append((
            pltpu.make_async_remote_copy(
                src_ref=terms.at[tile], dst_ref=terms.at[tile],
                send_sem=term_send.at[hop], recv_sem=term_recv.at[hop],
                device_id={"tile": lax.rem(tile + hop, tiles)}, device_id_type=MESH,
            ),
            pltpu.make_async_remote_copy(
                src_ref=terms.at[tile], dst_ref=terms.at[lax.rem(tile + tiles - hop, tiles)],
                send_sem=term_send.at[hop], recv_sem=term_recv.at[hop],
                device_id={"tile": lax.rem(tile + hop, tiles)}, device_id_type=MESH,
            ),
        ))
    for copy, _ in copies:
        copy.start()
    for t in range(STEPS):
        for group in (0, 1):
            for side in (0, 1):
                @pl.when(sends[side])
                def _():
                    for copy in halo(group, t, side):
                        copy.wait_send()
    for copy, arrival in copies:
        copy.wait_send()
        arrival.wait_recv()
    total = terms[0, 0:1]
    for other in range(1, tiles):
        total = total + terms[other, 0:1]
    misfit[0] = jnp.sum(total)


def per_device(tiles, state, parent, depth, interp, obs, counts):
    _, fields, levels, rows, cols = state.shape
    blocks = cols // 128
    tall = fields * levels * rows * blocks
    raw = state.reshape(fields * levels, rows, blocks, 128).transpose(0, 2, 1, 3).reshape(tall, 128)
    vmem, smem = pl.BlockSpec(memory_space=pltpu.VMEM), pl.BlockSpec(memory_space=pltpu.SMEM)
    forecast, misfit = pl.pallas_call(
        functools.partial(forecast_kernel, levels, tiles),
        out_shape=(
            jax.ShapeDtypeStruct((tall, 128), jnp.float32),
            jax.ShapeDtypeStruct((1,), jnp.float32),
        ),
        in_specs=[vmem, smem, vmem, vmem, smem],
        out_specs=(vmem, smem),
        scratch_shapes=[
            pltpu.VMEM((STEPS + 1, fields, levels, rows + 4, blocks, 128), jnp.float32),
            pltpu.VMEM((tiles, 8, 128), jnp.float32),
            pltpu.SemaphoreType.DMA((STEPS, 2, 2, 2)),
            pltpu.SemaphoreType.DMA((STEPS, 2, 2, 2)),
            pltpu.SemaphoreType.DMA((tiles,)),
            pltpu.SemaphoreType.DMA((tiles,)),
        ],
        compiler_params=pltpu.CompilerParams(
            collective_id=0, has_side_effects=True, vmem_limit_bytes=40 << 20
        ),
    )(raw, depth, interp[0], obs[0], counts)

    mine = parent[lax.axis_index("member")]
    everyone = lax.all_gather(forecast, "member", axis=0)
    selected = jnp.arange(everyone.shape[0], dtype=jnp.int32) == mine
    chosen = jnp.sum(jnp.where(selected[:, None, None], everyone, 0.0), axis=0)
    misfits = lax.all_gather(misfit, "member", axis=0, tiled=True)
    chosen_misfit = jnp.sum(jnp.where(selected, misfits, 0.0))
    result = chosen.reshape(fields * levels, blocks, rows, 128).transpose(0, 2, 1, 3)
    return result.reshape(state.shape), chosen_misfit.reshape(1)


def solution(mesh):
    return jax.shard_map(
        functools.partial(per_device, mesh.shape["tile"]),
        mesh=mesh,
        in_specs=(
            P(("parts", "member"), None, None, "tile", None),
            P("parts"),
            P(),
            P(("parts", "tile"), None, None),
            P(("parts", "tile"), None, None),
            P(("parts", "tile")),
        ),
        out_specs=(P(("parts", "member"), None, None, "tile", None), P(("parts", "member"))),
        check_vma=False,
    )
```

```python
import functools

import jax
import jax.numpy as jnp
from jax import lax
from jax.experimental import pallas as pl
from jax.experimental.pallas import tpu as pltpu
from jax.sharding import PartitionSpec as P

STEPS = 4
GROUPS = 4
U, H, V = 0, 1, 2
SOURCE = {U: 0, V: 1, H: 2}
MESH = pl.DeviceIdType.MESH

time_step = 0.3
nudge_gain = 2.0
coriolis = 0.5
viscosity = 0.05
mixing = 0.1


def west(field):
    turned = pltpu.roll(field, 1, 2)
    wrapped = pltpu.roll(turned, 1, 1)
    lane = lax.broadcasted_iota(jnp.int32, field.shape, 2)
    return jnp.where(lane == 0, wrapped, turned)


def east(field):
    turned = pltpu.roll(field, 127, 2)
    wrapped = pltpu.roll(turned, 7, 1)
    lane = lax.broadcasted_iota(jnp.int32, field.shape, 2)
    return jnp.where(lane == 127, wrapped, turned)


def forecast_kernel(
    levels, tiles, members,
    state, parent, depth, interp, obs, counts,
    out, misfit,
    x, done, inbox, outbox, terms, member_terms,
    send_sem, recv_sem, ship_send, ship_recv,
    term_send, term_recv, member_send, member_recv,
):
    tile = lax.axis_index("tile")
    right, left = lax.rem(tile + 1, tiles), lax.rem(tile + tiles - 1, tiles)
    barrier = pltpu.get_barrier_semaphore()
    for hop in range(1, tiles):
        pl.semaphore_signal(
            barrier, inc=1, device_id={"tile": lax.rem(tile + hop, tiles)}, device_id_type=MESH
        )

    me = lax.axis_index("member")
    for hop in range(1, members):
        pl.semaphore_signal(
            barrier, inc=1, device_id={"member": lax.rem(me + hop, members)}, device_id_type=MESH
        )

    ends = [levels * (GROUPS - g) // GROUPS for g in range(GROUPS + 1)]

    def span(group, t):
        low = 0 if group == GROUPS - 1 else ends[group + 1] - STEPS + t
        high = levels if group == 0 else ends[group] - STEPS + t
        return low, high

    def raw(f, l, r):
        return pl.ds((SOURCE[f] * levels + l) * 32 + r, 8, stride=4)

    def load(group):
        low, high = span(group, 0)

        @pl.loop(low, high)
        def _(l):
            for f in (U, H, V):
                for r in range(4):
                    x[0, f, l, 2 + r] = state[raw(f, l, r), :]

    def halo(group, t, side):
        low, high = span(group, t)
        lv = pl.ds(low, high - low)
        if side == 0:
            pieces = ((x.at[t, pl.ds(0, 2), lv, pl.ds(4, 2)], x.at[t, pl.ds(0, 2), lv, pl.ds(0, 2)]),
                      (x.at[t, V, lv, pl.ds(5, 1)], x.at[t, V, lv, pl.ds(1, 1)]))
            to = right
        else:
            pieces = ((x.at[t, pl.ds(0, 2), lv, pl.ds(2, 2)], x.at[t, pl.ds(0, 2), lv, pl.ds(6, 2)]),
                      (x.at[t, V, lv, pl.ds(2, 1)], x.at[t, V, lv, pl.ds(6, 1)]))
            to = left
        return [
            pltpu.make_async_remote_copy(
                src_ref=src, dst_ref=dst,
                send_sem=send_sem.at[t, group, side, i], recv_sem=recv_sem.at[t, group, side, i],
                device_id={"tile": to}, device_id_type=MESH,
            )
            for i, (src, dst) in enumerate(pieces)
        ]

    sends = (tile < tiles - 1, tile > 0)
    receives = (tile > 0, tile < tiles - 1)

    def send(group, t):
        for side in (0, 1):
            @pl.when(sends[side])
            def _():
                for copy in halo(group, t, side):
                    copy.start()

    def arrived(group, t):
        for side in (0, 1):
            @pl.when(receives[side])
            def _():
                for copy in halo(group, t, side):
                    copy.wait_recv()

    def cell(t, l, below, above):
        u, h = x[t, U, l], x[t, H, l]
        v = x[t, V, l, 1:7]
        core = u[1:7]
        u1 = (
            (1.0 - time_step * (4.0 * viscosity + 2.0 * mixing)) * core
            + (time_step * coriolis) * v
            - (time_step * 0.5) * (h[2:8] - h[0:6])
            + (time_step * viscosity) * ((u[2:8] + u[0:6]) + (west(core) + east(core)))
            + (time_step * mixing) * (x[t, U, below, 1:7] + x[t, U, above, 1:7])
        )
        mid = v[1:5]
        diffuse = (time_step * viscosity) * mid
        slope = (time_step * 0.5) * h[2:6]
        v1 = (
            (1.0 - time_step * (4.0 * viscosity + 2.0 * mixing)) * mid
            - (time_step * coriolis) * u[2:6]
            + (time_step * viscosity) * (v[2:6] + v[0:4])
            + (east(diffuse - slope) + west(diffuse + slope))
            + (time_step * mixing) * (x[t, V, below, 2:6] + x[t, V, above, 2:6])
        )
        h1 = h[2:6] - (time_step * 0.5 * depth[l]) * (
            (u1[2:6] - u1[0:4]) + (east(v1) - west(v1))
        )
        if t + 1 < STEPS:
            x[t + 1, U, l, 2:6] = u1[1:5]
            x[t + 1, V, l, 2:6] = v1
            x[t + 1, H, l, 2:6] = h1
        else:
            done[U, l] = u1[1:5]
            done[V, l] = v1
            done[H, l] = h1

    def advance(group, t):
        low, high = span(group, t + 1)
        if low == 0:
            cell(t, 0, 0, 1)
            low = 1
        last = high == levels
        if last:
            high = levels - 1

        @pl.loop(low, high)
        def _(l):
            cell(t, l, l - 1, l + 1)

        if last:
            cell(t, levels - 1, levels - 2, levels - 1)

    row = lax.broadcasted_iota(jnp.int32, (8, 128), 0)
    live = lax.broadcasted_iota(jnp.int32, (1, 128), 1) < counts[0]

    def residual(t):
        pieces = []
        for r in range(4):
            if t < STEPS:
                u, v = x[t, U, 0, 2 + r], x[t, V, 0, 2 + r]
            else:
                u, v = done[U, 0, r], done[V, 0, r]
            for block in range(8):
                here = row == block
                pieces.append(
                    jnp.concatenate([jnp.where(here, u, 0.0), jnp.where(here, v, 0.0)], axis=0)
                    .astype(jnp.bfloat16)
                )
        surf = jnp.concatenate(pieces, axis=1)
        pred = lax.dot_general(
            surf, interp[...], (((1,), (1,)), ((), ())), preferred_element_type=jnp.float32
        )
        result = []
        for k in (0, 1):
            whole = jnp.sum(pred[8 * k:8 * k + 8], axis=0, keepdims=True)
            result.append(jnp.where(live, obs[k:k + 1, :] - whole, 0.0))
        return result

    def nudge(t):
        innov = jnp.concatenate(
            [jnp.broadcast_to(part, (8, 128)) for part in residual(t)], axis=0
        ).astype(jnp.bfloat16)
        back = jnp.dot(innov, interp[...], preferred_element_type=jnp.float32)
        for k, f in ((0, U), (1, V)):
            for r in range(4):
                total = jnp.zeros((8, 128), jnp.float32)
                for block in range(8):
                    at = (r * 8 + block) * 128
                    total = jnp.where(row == block, back[8 * k:8 * k + 8, at:at + 128], total)
                x[t, f, 0, 2 + r] += (time_step * nudge_gain) * total

    half = members // 2
    place = (me, members - 1 - me)
    following = (lax.rem(me + 1, members), lax.rem(me + members - 1, members))

    def parent_place(way, place_of):
        return parent[place_of] if way == 0 else members - 1 - parent[members - 1 - place_of]

    def is_value(value, number):
        return jnp.broadcast_to((jnp.full((8, 128), value, jnp.int32) == number)[None], (4, 8, 128))

    def ship(way, source, slot, group):
        low, high = span(group, STEPS)
        lv = pl.ds(low, high - low)
        return pltpu.make_async_remote_copy(
            src_ref=source.at[:, lv], dst_ref=inbox.at[way, slot, :, lv],
            send_sem=ship_send.at[way, slot, group], recv_sem=ship_recv.at[way, slot, group],
            device_id={"member": following[way]}, device_id_type=MESH,
        )

    def ship_own(group):
        for way in (0, 1):
            @pl.when(place[way] < half)
            def _():
                ship(way, done, place[way], group).start()

    def relay(group):
        for way in (0, 1):
            @pl.when(place[way] < half)
            def _():
                @pl.loop(0, place[way])
                def _(slot):
                    ship(way, done, slot, group).wait_recv()
                    ship(way, inbox.at[way, slot], slot, group).start()

    def take(group):
        low, high = span(group, STEPS)
        for way in (0, 1):
            @pl.when(place[way] == half)
            def _():
                @pl.loop(0, half)
                def _(slot):
                    ship(way, done, slot, group).wait_recv()

                @pl.loop(half + 1, members)
                def _(receiver):
                    wanted = parent_place(way, receiver)
                    slot = receiver - half - 1
                    masks = [is_value(wanted, other) for other in range(half)]

                    @pl.loop(low, high)
                    def _(l):
                        for f in (U, H, V):
                            value = done[f, l]
                            for other in range(half):
                                value = jnp.where(masks[other], inbox[way, other, f, l], value)
                            outbox[way, slot, f, l] = value

                    ship(way, outbox.at[way, slot], slot, group).start()

            @pl.when(place[way] > half)
            def _():
                @pl.loop(place[way], members)
                def _(receiver):
                    ship(way, done, receiver - half - 1, group).wait_recv()

                @pl.loop(place[way] + 1, members)
                def _(receiver):
                    slot = receiver - half - 1
                    own = is_value(parent_place(way, receiver), place[way])

                    @pl.loop(low, high)
                    def _(l):
                        for f in (U, H, V):
                            outbox[way, slot, f, l] = jnp.where(
                                own, done[f, l], inbox[way, slot, f, l]
                            )

                    ship(way, outbox.at[way, slot], slot, group).start()

    def finish(group):
        low, high = span(group, STEPS)
        masks = []
        for way in (0, 1):
            wanted = parent_place(way, place[way])
            slot = jnp.where(
                wanted < place[way],
                jnp.where(place[way] <= half, wanted, place[way] - half - 1),
                -1,
            )
            masks += [(way, other, is_value(slot, other)) for other in range(half)]

        @pl.loop(low, high)
        def _(l):
            for f in (U, H, V):
                value = done[f, l]
                for way, other, mask in masks:
                    value = jnp.where(mask, inbox[way, other, f, l], value)
                for r in range(4):
                    out[raw(f, l, r), :] = value[r]

    def shipped(group):
        for way in (0, 1):
            @pl.when(place[way] < half)
            def _():
                @pl.loop(0, place[way] + 1)
                def _(slot):
                    ship(way, done, slot, group).wait_send()

            @pl.when(place[way] >= half)
            def _():
                @pl.loop(place[way] + 1, members)
                def _(receiver):
                    ship(way, done, receiver - half - 1, group).wait_send()

    for side, rows in ((0, 0), (1, 6)):
        @pl.when(jnp.logical_not(receives[side]))
        def _():
            @pl.loop(0, levels)
            def _(l):
                for t in range(STEPS):
                    for f in (U, H, V):
                        x[t, f, l, rows:rows + 2] = jnp.zeros((2, 8, 128), jnp.float32)

    load(0)
    pl.semaphore_wait(barrier, tiles + members - 2)
    send(0, 0)
    for group in range(1, GROUPS):
        load(group)
        if group == GROUPS - 1:
            nudge(0)
        send(group, 0)
    last = GROUPS + STEPS - 1
    for stage in range(last):
        for group in range(GROUPS):
            t = stage - group
            if 0 <= t < STEPS:
                arrived(group, t)
                advance(group, t)
                if t + 1 < STEPS:
                    if group == GROUPS - 1:
                        nudge(t + 1)
                    send(group, t + 1)
                else:
                    ship_own(group)
        ready = stage - STEPS - 1
        if ready >= 0:
            relay(ready)

    part_u, part_v = residual(STEPS)
    terms[pl.ds(tile, 1)] = jnp.broadcast_to(
        0.5 * (part_u * part_u + part_v * part_v), (1, 8, 128)
    )
    copies = []
    for hop in range(1, tiles):
        copies.append((
            pltpu.make_async_remote_copy(
                src_ref=terms.at[tile], dst_ref=terms.at[tile],
                send_sem=term_send.at[hop], recv_sem=term_recv.at[hop],
                device_id={"tile": lax.rem(tile + hop, tiles)}, device_id_type=MESH,
            ),
            pltpu.make_async_remote_copy(
                src_ref=terms.at[tile], dst_ref=terms.at[lax.rem(tile + tiles - hop, tiles)],
                send_sem=term_send.at[hop], recv_sem=term_recv.at[hop],
                device_id={"tile": lax.rem(tile + hop, tiles)}, device_id_type=MESH,
            ),
        ))
    for copy, _ in copies:
        copy.start()
    for group in range(last - STEPS - 1, GROUPS):
        relay(group)
    for copy, arrival in copies:
        copy.wait_send()
        arrival.wait_recv()
    total = terms[0, 0:1]
    for other in range(1, tiles):
        total = total + terms[other, 0:1]
    member_terms[pl.ds(me, 1)] = jnp.broadcast_to(total, (1, 8, 128))
    copies = []
    for hop in range(1, members):
        for origin in (me, lax.rem(me + members - hop, members)):
            copies.append(pltpu.make_async_remote_copy(
                src_ref=member_terms.at[me], dst_ref=member_terms.at[origin],
                send_sem=member_send.at[hop], recv_sem=member_recv.at[hop],
                device_id={"member": lax.rem(me + hop, members)}, device_id_type=MESH,
            ))
    for copy in copies[::2]:
        copy.start()
    for group in range(GROUPS):
        take(group)
        finish(group)
    for copy, arrival in zip(copies[::2], copies[1::2]):
        copy.wait_send()
        arrival.wait_recv()
    chosen = jnp.zeros((8, 128), jnp.float32)
    for other in range(members):
        mask = jnp.full((8, 128), parent[me], jnp.int32) == other
        chosen = jnp.where(mask, member_terms[other], chosen)
    misfit[0] = jnp.sum(chosen[0:1])
    for t in range(STEPS):
        for group in range(GROUPS):
            for side in (0, 1):
                @pl.when(sends[side])
                def _():
                    for copy in halo(group, t, side):
                        copy.wait_send()
    for group in range(GROUPS):
        shipped(group)


def per_device(tiles, members, state, parent, depth, interp, obs, counts):
    _, fields, levels, rows, cols = state.shape
    blocks = cols // 128
    tall = fields * levels * rows * blocks
    half = members // 2
    raw = state.reshape(fields * levels, rows, blocks, 128).transpose(0, 2, 1, 3).reshape(tall, 128)
    vmem, smem = pl.BlockSpec(memory_space=pltpu.VMEM), pl.BlockSpec(memory_space=pltpu.SMEM)
    whole = (fields, levels, rows, blocks, 128)
    dma = pltpu.SemaphoreType.DMA
    result, misfit = pl.pallas_call(
        functools.partial(forecast_kernel, levels, tiles, members),
        out_shape=(
            jax.ShapeDtypeStruct((tall, 128), jnp.float32),
            jax.ShapeDtypeStruct((1,), jnp.float32),
        ),
        in_specs=[vmem, smem, smem, vmem, vmem, smem],
        out_specs=(vmem, smem),
        scratch_shapes=[
            pltpu.VMEM((STEPS, fields, levels, rows + 4, blocks, 128), jnp.float32),
            pltpu.VMEM(whole, jnp.float32),
            pltpu.VMEM((2, half) + whole, jnp.float32),
            pltpu.VMEM((2, max(half - 1, 1)) + whole, jnp.float32),
            pltpu.VMEM((tiles, 8, 128), jnp.float32),
            pltpu.VMEM((members, 8, 128), jnp.float32),
            dma((STEPS, GROUPS, 2, 2)), dma((STEPS, GROUPS, 2, 2)),
            dma((2, half, GROUPS)), dma((2, half, GROUPS)),
            dma((tiles,)), dma((tiles,)),
            dma((members,)), dma((members,)),
        ],
        compiler_params=pltpu.CompilerParams(
            collective_id=0, has_side_effects=True, vmem_limit_bytes=56 << 20
        ),
    )(raw, parent, depth, interp[0], obs[0], counts)
    result = result.reshape(fields * levels, blocks, rows, 128).transpose(0, 2, 1, 3)
    return result.reshape(state.shape), misfit


def solution(mesh):
    return jax.shard_map(
        functools.partial(per_device, mesh.shape["tile"], mesh.shape["member"]),
        mesh=mesh,
        in_specs=(
            P(("parts", "member"), None, None, "tile", None),
            P("parts"),
            P(),
            P(("parts", "tile"), None, None),
            P(("parts", "tile"), None, None),
            P(("parts", "tile")),
        ),
        out_specs=(P(("parts", "member"), None, None, "tile", None), P(("parts", "member"))),
        check_vma=False,
    )
```

```python
import functools

import jax
import jax.numpy as jnp
from jax import lax
from jax.experimental import pallas as pl
from jax.experimental.pallas import tpu as pltpu
from jax.sharding import PartitionSpec as P

STEPS = 4
GROUPS = 4
PIECES = 2
BATCH = 4
U, H, V = 0, 1, 2
SOURCE = {U: 0, V: 1, H: 2}
MESH = pl.DeviceIdType.MESH

time_step = 0.3
nudge_gain = 2.0
coriolis = 0.5
viscosity = 0.05
mixing = 0.1


def west(field):
    turned = pltpu.roll(field, 1, 2)
    wrapped = pltpu.roll(turned, 1, 1)
    lane = lax.broadcasted_iota(jnp.int32, field.shape, 2)
    return jnp.where(lane == 0, wrapped, turned)


def east(field):
    turned = pltpu.roll(field, 127, 2)
    wrapped = pltpu.roll(turned, 7, 1)
    lane = lax.broadcasted_iota(jnp.int32, field.shape, 2)
    return jnp.where(lane == 127, wrapped, turned)


def forecast_kernel(
    levels, tiles, members,
    state, parent, depth, interp, obs, counts,
    out, misfit,
    x0, x1, x2, x3, done, inbox, outbox, terms, member_terms,
    send_sem, recv_sem, ship_send, ship_recv,
    term_send, term_recv, member_send, member_recv,
):
    x = (x0, x1, x2, x3)
    tile = lax.axis_index("tile")
    right, left = lax.rem(tile + 1, tiles), lax.rem(tile + tiles - 1, tiles)
    barrier = pltpu.get_barrier_semaphore()
    for hop in range(1, tiles):
        pl.semaphore_signal(
            barrier, inc=1, device_id={"tile": lax.rem(tile + hop, tiles)}, device_id_type=MESH
        )

    me = lax.axis_index("member")
    for hop in range(1, members):
        pl.semaphore_signal(
            barrier, inc=1, device_id={"member": lax.rem(me + hop, members)}, device_id_type=MESH
        )

    ends = [levels * (GROUPS - g) // GROUPS for g in range(GROUPS + 1)]

    def span(group, t):
        low = 0 if group == GROUPS - 1 else ends[group + 1] - STEPS + t
        high = levels if group == 0 else ends[group] - STEPS + t
        return low, high

    def raw(f, l, r):
        return pl.ds((SOURCE[f] * levels + l) * 32 + r, 8, stride=4)

    def load(group):
        low, high = span(group, 0)

        @pl.loop(low, high)
        def _(l):
            for f in (U, H, V):
                for r in range(4):
                    x0[f, l, 2 + r] = state[raw(f, l, r), :]

    def halo(group, t, side):
        low, high = span(group, t)
        lv = pl.ds(low, high - low)
        if side == 0:
            pieces = ((x[t].at[pl.ds(0, 2), lv, pl.ds(4, 2)], x[t].at[pl.ds(0, 2), lv, pl.ds(0, 2)]),
                      (x[t].at[V, lv, pl.ds(5, 1)], x[t].at[V, lv, pl.ds(1, 1)]))
            to = right
        else:
            pieces = ((x[t].at[pl.ds(0, 2), lv, pl.ds(2, 2)], x[t].at[pl.ds(0, 2), lv, pl.ds(6, 2)]),
                      (x[t].at[V, lv, pl.ds(2, 1)], x[t].at[V, lv, pl.ds(6, 1)]))
            to = left
        return [
            pltpu.make_async_remote_copy(
                src_ref=src, dst_ref=dst,
                send_sem=send_sem.at[t, group, side, i], recv_sem=recv_sem.at[t, group, side, i],
                device_id={"tile": to}, device_id_type=MESH,
            )
            for i, (src, dst) in enumerate(pieces)
        ]

    sends = (tile < tiles - 1, tile > 0)
    receives = (tile > 0, tile < tiles - 1)

    def send(group, t):
        for side in (0, 1):
            @pl.when(sends[side])
            def _():
                for copy in halo(group, t, side):
                    copy.start()

    def arrived(group, t):
        for side in (0, 1):
            @pl.when(receives[side])
            def _():
                for copy in halo(group, t, side):
                    copy.wait_recv()

    def cells(t, middle):
        now = x[t]
        us, vs = {}, {}
        for place, (l, _, _) in enumerate(middle):
            us[place], vs[place] = now[U, l], now[V, l, 1:7]
        edge = len(middle)
        (first, below, _), (final, _, above) = middle[0], middle[-1]
        us[-1] = us[0] if below is first else now[U, below]
        vs[-1] = vs[0] if below is first else now[V, below, 1:7]
        us[edge] = us[edge - 1] if above is final else now[U, above]
        vs[edge] = vs[edge - 1] if above is final else now[V, above, 1:7]
        results = []
        for place, (l, _, _) in enumerate(middle):
            u, h, v = us[place], now[H, l], vs[place]
            core = u[1:7]
            u1 = (
                (1.0 - time_step * (4.0 * viscosity + 2.0 * mixing)) * core
                + (time_step * coriolis) * v
                - (time_step * 0.5) * (h[2:8] - h[0:6])
                + (time_step * viscosity) * ((u[2:8] + u[0:6]) + (west(core) + east(core)))
                + (time_step * mixing) * (us[place - 1][1:7] + us[place + 1][1:7])
            )
            mid = v[1:5]
            diffuse = (time_step * viscosity) * mid
            slope = (time_step * 0.5) * h[2:6]
            v1 = (
                (1.0 - time_step * (4.0 * viscosity + 2.0 * mixing)) * mid
                - (time_step * coriolis) * u[2:6]
                + (time_step * viscosity) * (v[2:6] + v[0:4])
                + (east(diffuse - slope) + west(diffuse + slope))
                + (time_step * mixing) * (vs[place - 1][1:5] + vs[place + 1][1:5])
            )
            results.append((l, u1, v1, h[2:6]))
        results = [
            (l, u1[1:5], v1, h - (time_step * 0.5 * depth[l]) * (
                (u1[2:6] - u1[0:4]) + (east(v1) - west(v1))
            ))
            for l, u1, v1, h in results
        ]
        for l, u1, v1, h1 in results:
            if t + 1 < STEPS:
                x[t + 1][U, l, 2:6] = u1
                x[t + 1][V, l, 2:6] = v1
                x[t + 1][H, l, 2:6] = h1
            else:
                done[U, l] = u1
                done[V, l] = v1
                done[H, l] = h1

    def advance(group, t):
        low, high = span(group, t + 1)

        def neighbours(l):
            if isinstance(l, int):
                return l, max(l - 1, 0) if l else l, l if l == levels - 1 else l + 1
            return l, l - 1, l + 1

        count = high - low
        whole = count // BATCH
        odd = count - whole * BATCH
        batches = [list(range(low + i * BATCH, low + (i + 1) * BATCH)) for i in range(whole)]
        if odd:
            batches.append(list(range(high - odd, high)))
        inner = [i for i in range(whole) if batches[i][0] > 0 and batches[i][-1] < levels - 1]
        for i, batch in enumerate(batches):
            if i not in inner or len(inner) < 2:
                cells(t, [neighbours(l) for l in batch])
        if len(inner) >= 2:
            @pl.loop(inner[0], inner[-1] + 1)
            def _(i):
                base = low + i * BATCH
                cells(t, [neighbours(base + j) for j in range(BATCH)])

    row = lax.broadcasted_iota(jnp.int32, (8, 128), 0)
    live = lax.broadcasted_iota(jnp.int32, (1, 128), 1) < counts[0]

    def residual(t):
        pieces = []
        for r in range(4):
            if t < STEPS:
                u, v = x[t][U, 0, 2 + r], x[t][V, 0, 2 + r]
            else:
                u, v = done[U, 0, r], done[V, 0, r]
            for block in range(8):
                here = row == block
                pieces.append(
                    jnp.concatenate([jnp.where(here, u, 0.0), jnp.where(here, v, 0.0)], axis=0)
                    .astype(jnp.bfloat16)
                )
        surf = jnp.concatenate(pieces, axis=1)
        pred = lax.dot_general(
            surf, interp[...], (((1,), (1,)), ((), ())), preferred_element_type=jnp.float32
        )
        result = []
        for k in (0, 1):
            whole = jnp.sum(pred[8 * k:8 * k + 8], axis=0, keepdims=True)
            result.append(jnp.where(live, obs[k:k + 1, :] - whole, 0.0))
        return result

    def nudge(t):
        innov = jnp.concatenate(
            [jnp.broadcast_to(part, (8, 128)) for part in residual(t)], axis=0
        ).astype(jnp.bfloat16)
        back = jnp.dot(innov, interp[...], preferred_element_type=jnp.float32)
        for k, f in ((0, U), (1, V)):
            for r in range(4):
                total = jnp.zeros((8, 128), jnp.float32)
                for block in range(8):
                    at = (r * 8 + block) * 128
                    total = jnp.where(row == block, back[8 * k:8 * k + 8, at:at + 128], total)
                x[t][f, 0, 2 + r] += (time_step * nudge_gain) * total

    half = members // 2
    place = (me, members - 1 - me)
    following = (lax.rem(me + 1, members), lax.rem(me + members - 1, members))

    def parent_place(way, place_of):
        return parent[place_of] if way == 0 else members - 1 - parent[members - 1 - place_of]

    def is_value(value, number):
        return jnp.broadcast_to((jnp.full((8, 128), value, jnp.int32) == number)[None], (4, 8, 128))

    def pieces_of(group):
        return range(group * PIECES, (group + 1) * PIECES)

    def bounds(piece):
        low, high = span(piece // PIECES, STEPS)
        count, part = high - low, PIECES - 1 - piece % PIECES
        return low + count * part // PIECES, low + count * (part + 1) // PIECES

    def ship(way, source, slot, piece):
        low, high = bounds(piece)
        lv = pl.ds(low, high - low)
        return pltpu.make_async_remote_copy(
            src_ref=source.at[:, lv], dst_ref=inbox.at[way, slot, :, lv],
            send_sem=ship_send.at[way, slot, piece], recv_sem=ship_recv.at[way, slot, piece],
            device_id={"member": following[way]}, device_id_type=MESH,
        )

    def ship_own(piece):
        for way in (0, 1):
            @pl.when(place[way] < half)
            def _():
                ship(way, done, place[way], piece).start()

    def relay(piece):
        for way in (0, 1):
            @pl.when(place[way] < half)
            def _():
                @pl.loop(0, place[way])
                def _(slot):
                    ship(way, done, slot, piece).wait_recv()
                    ship(way, inbox.at[way, slot], slot, piece).start()

    def take(piece):
        low, high = bounds(piece)
        for way in (0, 1):
            @pl.when(place[way] == half)
            def _():
                @pl.loop(0, half)
                def _(slot):
                    ship(way, done, slot, piece).wait_recv()

                @pl.loop(half + 1, members)
                def _(receiver):
                    wanted = parent_place(way, receiver)
                    slot = receiver - half - 1
                    masks = [is_value(wanted, other) for other in range(half)]

                    @pl.loop(low, high)
                    def _(l):
                        for f in (U, H, V):
                            value = done[f, l]
                            for other in range(half):
                                value = jnp.where(masks[other], inbox[way, other, f, l], value)
                            outbox[way, slot, f, l] = value

                    ship(way, outbox.at[way, slot], slot, piece).start()

            @pl.when(place[way] > half)
            def _():
                @pl.loop(place[way], members)
                def _(receiver):
                    ship(way, done, receiver - half - 1, piece).wait_recv()

                @pl.loop(place[way] + 1, members)
                def _(receiver):
                    slot = receiver - half - 1
                    own = is_value(parent_place(way, receiver), place[way])

                    @pl.loop(low, high)
                    def _(l):
                        for f in (U, H, V):
                            outbox[way, slot, f, l] = jnp.where(
                                own, done[f, l], inbox[way, slot, f, l]
                            )

                    ship(way, outbox.at[way, slot], slot, piece).start()

    def finish(piece):
        low, high = bounds(piece)
        masks = []
        for way in (0, 1):
            wanted = parent_place(way, place[way])
            slot = jnp.where(
                wanted < place[way],
                jnp.where(place[way] <= half, wanted, place[way] - half - 1),
                -1,
            )
            masks += [(way, other, is_value(slot, other)) for other in range(half)]

        @pl.loop(low, high)
        def _(l):
            for f in (U, H, V):
                value = done[f, l]
                for way, other, mask in masks:
                    value = jnp.where(mask, inbox[way, other, f, l], value)
                for r in range(4):
                    out[raw(f, l, r), :] = value[r]

    def shipped(piece):
        for way in (0, 1):
            @pl.when(place[way] < half)
            def _():
                @pl.loop(0, place[way] + 1)
                def _(slot):
                    ship(way, done, slot, piece).wait_send()

            @pl.when(place[way] >= half)
            def _():
                @pl.loop(place[way] + 1, members)
                def _(receiver):
                    ship(way, done, receiver - half - 1, piece).wait_send()

    for side, rows in ((0, 0), (1, 6)):
        @pl.when(jnp.logical_not(receives[side]))
        def _():
            @pl.loop(0, levels)
            def _(l):
                for t in range(STEPS):
                    for f in (U, H, V):
                        x[t][f, l, rows:rows + 2] = jnp.zeros((2, 8, 128), jnp.float32)

    load(0)
    pl.semaphore_wait(barrier, tiles + members - 2)
    send(0, 0)
    for group in range(1, GROUPS):
        load(group)
        if group == GROUPS - 1:
            nudge(0)
        send(group, 0)
    last = GROUPS + STEPS - 1
    for stage in range(last):
        for group in range(GROUPS):
            t = stage - group
            if 0 <= t < STEPS:
                arrived(group, t)
                advance(group, t)
                if t + 1 < STEPS:
                    if group == GROUPS - 1:
                        nudge(t + 1)
                    send(group, t + 1)
                else:
                    for piece in pieces_of(group):
                        ship_own(piece)
        if stage >= STEPS:
            for piece in pieces_of(stage - STEPS):
                relay(piece)

    part_u, part_v = residual(STEPS)
    terms[pl.ds(tile, 1)] = jnp.broadcast_to(
        0.5 * (part_u * part_u + part_v * part_v), (1, 8, 128)
    )
    copies = []
    for hop in range(1, tiles):
        copies.append((
            pltpu.make_async_remote_copy(
                src_ref=terms.at[tile], dst_ref=terms.at[tile],
                send_sem=term_send.at[hop], recv_sem=term_recv.at[hop],
                device_id={"tile": lax.rem(tile + hop, tiles)}, device_id_type=MESH,
            ),
            pltpu.make_async_remote_copy(
                src_ref=terms.at[tile], dst_ref=terms.at[lax.rem(tile + tiles - hop, tiles)],
                send_sem=term_send.at[hop], recv_sem=term_recv.at[hop],
                device_id={"tile": lax.rem(tile + hop, tiles)}, device_id_type=MESH,
            ),
        ))
    for copy, _ in copies:
        copy.start()
    for group in range(last - STEPS, GROUPS):
        for piece in pieces_of(group):
            relay(piece)
    for copy, arrival in copies:
        copy.wait_send()
        arrival.wait_recv()
    total = terms[0, 0:1]
    for other in range(1, tiles):
        total = total + terms[other, 0:1]
    member_terms[pl.ds(me, 1)] = jnp.broadcast_to(total, (1, 8, 128))
    copies = []
    for hop in range(1, members):
        for origin in (me, lax.rem(me + members - hop, members)):
            copies.append(pltpu.make_async_remote_copy(
                src_ref=member_terms.at[me], dst_ref=member_terms.at[origin],
                send_sem=member_send.at[hop], recv_sem=member_recv.at[hop],
                device_id={"member": lax.rem(me + hop, members)}, device_id_type=MESH,
            ))
    for copy in copies[::2]:
        copy.start()
    for piece in range(GROUPS * PIECES):
        take(piece)
        finish(piece)
    for copy, arrival in zip(copies[::2], copies[1::2]):
        copy.wait_send()
        arrival.wait_recv()
    chosen = jnp.zeros((8, 128), jnp.float32)
    for other in range(members):
        mask = jnp.full((8, 128), parent[me], jnp.int32) == other
        chosen = jnp.where(mask, member_terms[other], chosen)
    misfit[0] = jnp.sum(chosen[0:1])
    for t in range(STEPS):
        for group in range(GROUPS):
            for side in (0, 1):
                @pl.when(sends[side])
                def _():
                    for copy in halo(group, t, side):
                        copy.wait_send()
    for piece in range(GROUPS * PIECES):
        shipped(piece)


def per_device(tiles, members, state, parent, depth, interp, obs, counts):
    _, fields, levels, rows, cols = state.shape
    blocks = cols // 128
    tall = fields * levels * rows * blocks
    half = members // 2
    raw = state.reshape(fields * levels, rows, blocks, 128).transpose(0, 2, 1, 3).reshape(tall, 128)
    vmem, smem = pl.BlockSpec(memory_space=pltpu.VMEM), pl.BlockSpec(memory_space=pltpu.SMEM)
    whole = (fields, levels, rows, blocks, 128)
    dma = pltpu.SemaphoreType.DMA
    result, misfit = pl.pallas_call(
        functools.partial(forecast_kernel, levels, tiles, members),
        out_shape=(
            jax.ShapeDtypeStruct((tall, 128), jnp.float32),
            jax.ShapeDtypeStruct((1,), jnp.float32),
        ),
        in_specs=[vmem, smem, smem, vmem, vmem, smem],
        out_specs=(vmem, smem),
        scratch_shapes=[
            *[pltpu.VMEM((fields, levels, rows + 4, blocks, 128), jnp.float32)] * STEPS,
            pltpu.VMEM(whole, jnp.float32),
            pltpu.VMEM((2, half) + whole, jnp.float32),
            pltpu.VMEM((2, max(half - 1, 1)) + whole, jnp.float32),
            pltpu.VMEM((tiles, 8, 128), jnp.float32),
            pltpu.VMEM((members, 8, 128), jnp.float32),
            dma((STEPS, GROUPS, 2, 2)), dma((STEPS, GROUPS, 2, 2)),
            dma((2, half, GROUPS * PIECES)), dma((2, half, GROUPS * PIECES)),
            dma((tiles,)), dma((tiles,)),
            dma((members,)), dma((members,)),
        ],
        compiler_params=pltpu.CompilerParams(
            collective_id=0, has_side_effects=True, vmem_limit_bytes=56 << 20
        ),
    )(raw, parent, depth, interp[0], obs[0], counts)
    result = result.reshape(fields * levels, blocks, rows, 128).transpose(0, 2, 1, 3)
    return result.reshape(state.shape), misfit


def solution(mesh):
    return jax.shard_map(
        functools.partial(per_device, mesh.shape["tile"], mesh.shape["member"]),
        mesh=mesh,
        in_specs=(
            P(("parts", "member"), None, None, "tile", None),
            P("parts"),
            P(),
            P(("parts", "tile"), None, None),
            P(("parts", "tile"), None, None),
            P(("parts", "tile")),
        ),
        out_specs=(P(("parts", "member"), None, None, "tile", None), P(("parts", "member"))),
        check_vma=False,
    )
```
